512 devices in a mesh: expert: 128 (over z, x, core), hidden: 4 (over y).
Axes of the slice: x: 4, y: 4, z: 16, core: 2. Of those that a mesh axis runs over, the one named last changes fastest.
Arguments:
- tokens: bfloat16 [2048, 4096], P('expert', 'hidden'), may hold values from -6 to 6
- expert_ids: int32 [2048, 8], P('expert'), may hold values from 0 to 127, all different within a row; in each aligned block of 16 rows (0 to 15, 16 to 31, ...) at most 2 rows name the same one
- route_probs: float32 [2048, 8], P('expert'), may hold values from 0.02 to 1
- gate_weight: bfloat16 [128, 768, 4096], P('expert', 'hidden'), may hold values from -0.09375 to 0.09375
- up_weight: bfloat16 [128, 768, 4096], P('expert', 'hidden'), may hold values from -0.09375 to 0.09375
- down_weight: bfloat16 [128, 768, 4096], P('expert', 'hidden'), may hold values from -0.21875 to 0.21875
Outputs:
- layer_out: bfloat16 [2048, 4096], P('expert', 'hidden')
The draws below stay inside these ranges and needn't reach their ends.
Inputs may be any that keep to these rules, and one draw needn't show every extreme that they name: `expert_ids`: among the 16 tokens of one index of the expert axis no expert is named more than 2 times, a bound that some block reaches; a token's 8 ids differ.
All inputs are finite; a program needn't handle non-finite values.
Results may differ from the reference program's by a relative error of at most 0.015.
Values may be sent and summed in bfloat16 or wider, within the bound.
A program may use at most 64 MiB of HBM per device.

```python
import math
import jax
import jax.numpy as jnp
import numpy as np
from jax import lax

D = 4096
HID = 768
TOP = 8
TOK_DEV = 16
EXPERTS = 128
CAP = 2
HQ = 192
TOKENS = 2048
N_EXPERT = 128
N_HIDDEN = 4


def steps_of(stream_key, extent, pieces, least, high):
    def one(position, shards_of):
        heights = jax.random.uniform(jax.random.fold_in(jax.random.fold_in(stream_key, 6), position), (shards_of,), jnp.float32, least / len(pieces), high / len(pieces))
        return jnp.repeat(jnp.exp(heights), extent[position] // shards_of).reshape((-1,) + (1,) * (len(extent) - position - 1))

    level = one(*pieces[0])
    for cut in pieces[1:]:
        level = level * one(*cut)
    return level


def deal_out(stream_key, own, number, rows, number_of, top, reach, skew):
    ranking = jax.random.permutation(stream_key, number_of)
    packed, ordinary = load_shares(number_of, rows * top, reach, skew, True), load_shares(number_of, rows * top, reach, skew, False)
    places = jnp.arange(number_of)

    def named(tallies, offset_by):
        used = int((tallies > 0).sum())
        fixed = max(1, used // 4)
        moved = fixed + (places - fixed + offset_by * (used - fixed)) % max(1, number_of - fixed)
        return jnp.zeros((number_of,), jnp.int32).at[ranking[jnp.where(places < fixed, places, moved)]].set(jnp.asarray(tallies, jnp.int32))

    tallies = jnp.where(number % 4 == 0, named(packed, number // 4), named(ordinary, number - number // 4 - 1))
    mixed = jax.random.permutation(jax.random.fold_in(own, 3), number_of)
    giver, taker = mixed[0:number_of // 2 * 2:2], mixed[1:number_of // 2 * 2:2]
    room = jnp.minimum(tallies[giver] - 1, reach - tallies[taker]) // 2
    room = jnp.where((giver == ranking[0]) | (taker == ranking[0]) | (tallies[taker] == 0), 0, jnp.maximum(room, 0))
    moved = jax.random.randint(jax.random.fold_in(own, 4), (number_of // 2,), 0, 1 << 20) % (room + 1)
    tallies = tallies.at[giver].add(-moved).at[taker].add(moved)
    labels = jnp.searchsorted(jnp.cumsum(tallies), jnp.arange(rows * top), side="right").astype(jnp.int32)
    listing = labels.reshape(top, rows).T
    listing = listing[jax.random.permutation(jax.random.fold_in(own, 1), rows)]
    offset_by = jax.random.randint(jax.random.fold_in(own, 2), (rows, 1), 0, top)
    return jnp.take_along_axis(listing, (jnp.arange(top)[None, :] + offset_by) % top, axis=1)


def load_shares(number_of, total, bound, slope, full):
    loads = [(1 << 20) // math.isqrt(grade ** slope) + 1 for grade in range(1, number_of + 1)]
    largest = bound if full else min(bound, max(-(-total // number_of), total * loads[0] // sum(loads)))
    least = 1 if total - largest >= number_of - 1 else 0
    given, rest = [largest] + [least] * (number_of - 1), total - largest - least * (number_of - 1)
    while rest > 0:
        candidates = [i for i in range(1, number_of) if given[i] < largest] or [i for i in range(1, number_of) if given[i] < bound]
        pool, remaining = sum([loads[i] for i in candidates]), rest
        for i in candidates:
            addition = min(bound - given[i], max(1, remaining * loads[i] // pool), rest)
            given[i] = given[i] + addition
            rest = rest - addition
    return np.array(given)


def normal_values(own_key, shape, spread, limit, split=(), kind=jnp.bfloat16):
    values = spread * jax.random.normal(own_key, shape, jnp.float32)
    if split:
        values = values * steps_of(own_key, shape, split, -0.22, 0.18)
    return jnp.clip(values, -limit, limit).astype(kind)


def setup_inputs(seed: int = 0) -> dict:
    key_of = jax.random.split(jax.random.key(seed), 7)
    tokens = normal_values(key_of[0], (TOKENS, D), 1.0, 6.0, ((0, 128), (1, 4)))
    expert_ids_keys = jax.random.split(jax.random.fold_in(key_of[1], 1), TOKENS // TOK_DEV)
    expert_ids_turns = jax.random.permutation(jax.random.fold_in(key_of[1], 3), TOKENS // TOK_DEV)
    expert_ids = jax.vmap(lambda own, number: deal_out(jax.random.fold_in(key_of[1], 2), own, number, TOK_DEV, EXPERTS, TOP, CAP, 2))(expert_ids_keys, expert_ids_turns).reshape((TOKENS, TOP))
    route_probs = jnp.clip(jnp.exp(math.log(1.0) - 3.912023 * jax.random.uniform(key_of[2], (TOKENS, TOP), jnp.float32) ** steps_of(key_of[2], (TOKENS, TOP), ((0, 128),), -0.2, 0.2)), 0.02, 1.0)
    gate_weight = normal_values(key_of[3], (EXPERTS, HID, D), D ** -0.5, 0.09375, ((0, 128), (1, 4)))
    up_weight = normal_values(key_of[4], (EXPERTS, HID, D), D ** -0.5, 0.09375, ((0, 128), (1, 4)))
    down_weight = normal_values(key_of[5], (EXPERTS, HID, D), HID ** -0.5, 0.21875, ((0, 128), (1, 4)))
    return {"tokens": tokens, "expert_ids": expert_ids, "route_probs": route_probs, "gate_weight": gate_weight, "up_weight": up_weight, "down_weight": down_weight}


def reference(tokens, expert_ids, route_probs, gate_weight, up_weight, down_weight):
    weights = route_probs / jnp.sum(route_probs, axis=1, keepdims=True)
    flat_ids = expert_ids.reshape(-1)
    flat_weights = weights.reshape(-1)
    most_rows = N_EXPERT * CAP
    contract = (((1,), (1,)), ((), ()))

    def one_expert(total, expert):
        chosen = flat_ids == expert
        live_count = jnp.sum(chosen.astype(jnp.int32))
        picked = jnp.nonzero(chosen, size=most_rows, fill_value=0)[0].astype(jnp.int32)
        valid = jnp.arange(most_rows, dtype=jnp.int32) < live_count
        token_rows = (picked // TOP).astype(jnp.int32)
        row_data = tokens[token_rows]
        gate_out = lax.dot_general(row_data, gate_weight[expert], contract, preferred_element_type=jnp.float32)
        up_out = lax.dot_general(row_data, up_weight[expert], contract, preferred_element_type=jnp.float32)
        activated = (jax.nn.silu(gate_out) * up_out).astype(jnp.bfloat16)
        down_rows = down_weight[expert]
        summed = jnp.zeros((most_rows, D), jnp.float32)
        for hidden_block in range(N_HIDDEN):
            piece_sum = jnp.dot(activated[:, hidden_block * HQ:(hidden_block + 1) * HQ],
                                down_rows[hidden_block * HQ:(hidden_block + 1) * HQ],
                                preferred_element_type=jnp.float32)
            rounded = lax.optimization_barrier(piece_sum.astype(jnp.bfloat16))
            summed = summed + rounded.astype(jnp.float32)
        row_weight = jnp.where(valid, flat_weights[picked], jnp.float32(0.0))
        total = total.at[token_rows].add(row_weight[:, None] * summed)
        return total, None

    total = lax.scan(one_expert, jnp.zeros((TOKENS, D), jnp.float32),
                     jnp.arange(EXPERTS, dtype=jnp.int32))[0]
    return total.astype(jnp.bfloat16)
```

```python
import jax
import jax.numpy as jnp
from jax import lax
from jax.experimental import pallas as pl
from jax.experimental.pallas import tpu as pltpu
from jax.sharding import PartitionSpec as P

MESH = pl.DeviceIdType.MESH
BF16 = jnp.bfloat16
F32 = jnp.float32
NZ, NXC, NY = 16, 8, 4
NEAR = 32
GROUPS = ((0,), (1,), (3,), (2,))
BASE = (0, 64, 128, 192)
ROWS = (64, 64, 64, 64)
EXPERT = ((0,), (1,), (2,), (3,))
ORDER = (
    ("h", 0), ("a", 0), ("p", 0), ("b", 0), ("a", 1), ("a", 2), ("c", 0), ("b", 1), ("a", 3), ("b", 2),
    ("c", 1), ("w", 0), ("b", 3), ("c", 2), ("d", 1), ("c", 3), ("d", 2), ("e", 1), ("d", 3), ("e", 2),
    ("f", 1), ("d", 0), ("e", 3), ("f", 2), ("e", 0), ("f", 3), ("g", 1), ("g", 2), ("f", 0), ("g", 3),
    ("g", 0),
)


def kernel(tok_hbm, ids_hbm, prob_hbm, gate_hbm, up_hbm, down_hbm, out_ref, *scratch):
    (tok, ids_ref, prob_ref, gate, up, down, far, wanted, perm, perm_back, weighted, xf, pf, step1, step2,
     part_out, part_in, in_sem, far_s, far_r, near_s, near_r, y_s, y_r, one_s, one_r, two_s, two_r,
     back_s, back_r, part_s, part_r) = scratch[:32]
    n = len(GROUPS)
    picked, got, back_out, back_in = (scratch[32 + n * i : 32 + n * i + n] for i in range(4))

    e = lax.axis_index("expert")
    y = lax.axis_index("hidden")
    z, xc = lax.div(e, NXC), lax.rem(e, NXC)
    two = jnp.where(lax.rem(z, 4) < 2, 2, NZ - 2)

    def along_y(dy):
        return (e, lax.rem(y + dy, NY))

    def along_z(dz):
        return (lax.rem(z + dz, NZ) * NXC + xc, y)

    z_bases = [lax.rem(z + dz, NZ) * NXC for dz in (0, 1, NZ - 1, two)]
    xcs = [lax.rem(xc + d, NXC) for d in range(NXC)]

    def ahead(j):
        return (z_bases[j // 8] + xcs[j % 8], y)

    def behind(j):
        return (z_bases[(0, 2, 1, 3)[j // 8]] + xcs[-j % 8], y)

    barrier = pltpu.get_barrier_semaphore()
    partners = [along_z(4 * k) for k in (1, 3, 2)]
    partners += [ahead(j) for j in range(NEAR - 1, 0, -1)]
    partners += [along_y(k) for k in range(1, NY)]
    inputs = [
        pltpu.make_async_copy(src, dst, in_sem.at[i])
        for i, (src, dst) in enumerate((
            (tok_hbm, tok), (ids_hbm, ids_ref), (prob_hbm, prob_ref),
            (gate_hbm.at[0], gate), (up_hbm.at[0], up), (down_hbm.at[0], down),
        ))
    ]
    for i in range(3):
        inputs[i].start()
    for partner in partners:
        pl.semaphore_signal(barrier, inc=1, device_id=partner, device_id_type=MESH)

    def remote(src, dst, send, recv, device):
        copy = pltpu.make_async_remote_copy(
            src_ref=src, dst_ref=dst, send_sem=send, recv_sem=recv,
            device_id=device, device_id_type=MESH,
        )
        copy.start()
        return copy

    def iota(shape, axis):
        return lax.broadcasted_iota(jnp.int32, shape, axis)

    nt = (((1,), (1,)), ((), ()))

    for i in range(3):
        inputs[i].wait()
    for group in range(8):
        far[0, 16 * group : 16 * group + 16, :] = tok[:, 128 * group : 128 * group + 128]
    probs = prob_ref[...]
    share = probs / jnp.sum(probs, axis=0, keepdims=True)
    lists = jnp.concatenate([ids_ref[...].astype(F32), share, jnp.zeros((112, 16), F32)], axis=0).astype(BF16)
    same = (iota((16, 16), 0) == iota((16, 16), 1)).astype(F32).astype(BF16)
    far[0, 128:144, :] = lax.dot_general(same, lists, nt, preferred_element_type=F32).astype(BF16)

    pl.semaphore_wait(barrier, len(partners))

    far_copies = {}

    def send_far(_):
        for k in (1, 3, 2):
            far_copies[k] = remote(far.at[0], far.at[k], far_s.at[k], far_r.at[k], along_z(4 * k))

    for i in range(3, 6):
        inputs[i].start()

    row, col = iota((512, 256), 0), iota((512, 256), 1)
    hop = row >> 7
    dz = jnp.where(hop == 0, 0, jnp.where(hop == 1, 1, jnp.where(hop == 2, NZ - 1, two)))
    target = ((z + dz) & 15) * NXC + ((xc + (row >> 4)) & 7) + ((row & 1) << 7)
    wanted[...] = (target == col).astype(F32).astype(BF16)
    same_group = ((iota((512, 128), 0) & 15) >> 1) == (iota((512, 128), 1) >> 4)

    lane = iota((16, 128), 1).astype(F32)
    below = (iota((16, 16), 0) > iota((16, 16), 1)).astype(F32).astype(BF16)

    def turns(k, weigh):
        lists = far[k, 128:144, :].astype(F32)
        named, value = jnp.zeros((16, 128), F32), jnp.zeros((16, 128), F32)
        for q in range(8):
            hit = lists[:, q : q + 1] == lane
            named = jnp.where(hit, 1.0, named)
            if weigh:
                value = jnp.where(hit, lists[:, 8 + q : 9 + q], value)
        rank = jnp.dot(below, named.astype(BF16), preferred_element_type=F32)
        what = value if weigh else named
        return jnp.concatenate([jnp.where(rank == 0.0, what, 0.0), jnp.where(rank == 1.0, what, 0.0)], axis=1)

    def spread(block):
        return jnp.concatenate([block] * 8, axis=0).astype(BF16)

    def select_and_send(g):
        for i, k in enumerate(GROUPS[g]):
            if k:
                far_copies[k].wait_recv()
            chosen = lax.dot_general(wanted[...], spread(turns(k, False)), nt, preferred_element_type=F32)
            chosen = jnp.where(same_group, chosen, 0.0).astype(BF16)
            picked[g][:, 128 * i : 128 * i + 128] = jnp.dot(
                chosen, far[k, 0:128, :], preferred_element_type=F32
            ).astype(BF16)
        for j in range(NEAR - 1, 0, -1):
            remote(
                picked[g].at[pl.ds(16 * j, 16)], got[g].at[pl.ds(16 * j, 16)],
                near_s.at[g], near_r.at[g], ahead(j),
            )
        got[g][0:16, :] = picked[g][0:16, :]

    def permutations(_):
        a, b = iota((512, 512), 0), iota((512, 512), 1)
        perm[...] = (b == (((a & 63) >> 1) << 4) + ((a >> 6) << 1) + (a & 1)).astype(F32).astype(BF16)
        perm_back[...] = (a == (((b & 63) >> 1) << 4) + ((b >> 6) << 1) + (b & 1)).astype(F32).astype(BF16)

    def weights(_):
        for i in range(3, 6):
            inputs[i].wait()
        same = (iota((128, 512), 0) >> 4) == ((iota((128, 512), 1) & 15) >> 1)
        for k in range(4):
            full = lax.dot_general(spread(turns(k, True)), wanted[...], nt, preferred_element_type=F32)
            weighted[k] = jnp.where(same, full, 0.0).astype(BF16)

    def wait_all(ref, sem):
        rest = ref.at[pl.ds(16, 496)]
        pltpu.make_async_copy(rest, rest, sem).wait()

    y_copies, one_copies, two_copies, part_copies = {}, {}, {}, {}

    def send_y(g):
        wait_all(got[g], near_r.at[g])
        rows = jnp.dot(perm[...], got[g][...], preferred_element_type=F32).astype(BF16)
        for i in range(len(GROUPS[g])):
            first = BASE[g] + 64 * i
            for group in range(8):
                xf[y, first : first + 64, 128 * group : 128 * group + 128] = rows[
                    64 * group : 64 * group + 64, 128 * i : 128 * i + 128
                ]
        block = xf.at[y, pl.ds(BASE[g], ROWS[g])]
        y_copies[g, 0] = remote(block, block, y_s.at[g, 0], y_r.at[g, 0], along_y(1))
        y_copies[g, 1] = remote(block, block, y_s.at[g, 1], y_r.at[g, 1], along_y(3))

    def first_half(g):
        return pl.ds(BASE[g], ROWS[g] // 2)

    def second_half(g):
        return pl.ds(BASE[g] + ROWS[g] // 2, ROWS[g] // 2)

    def forward_y(g):
        y_copies[g, 0].wait_recv()
        block = xf.at[lax.rem(y + 3, NY), first_half(g)]
        y_copies[g, 2] = remote(block, block, y_s.at[g, 2], y_r.at[g, 2], along_y(1))
        y_copies[g, 1].wait_recv()
        block = xf.at[lax.rem(y + 1, NY), second_half(g)]
        y_copies[g, 3] = remote(block, block, y_s.at[g, 3], y_r.at[g, 3], along_y(3))

    def expert(which):
        members = EXPERT[which]
        for g in members:
            y_copies[g, 2].wait_recv()
            y_copies[g, 3].wait_recv()
        count = sum(ROWS[g] for g in members)
        rows = pl.ds(BASE[members[0]], count)
        gate_out, up_out = jnp.zeros((count, 192), F32), jnp.zeros((count, 192), F32)
        for q in range(NY):
            x = xf[q, rows, :]
            gate_out += lax.dot_general(x, gate[:, 1024 * q : 1024 * q + 1024], nt, preferred_element_type=F32)
            up_out += lax.dot_general(x, up[:, 1024 * q : 1024 * q + 1024], nt, preferred_element_type=F32)
        hidden = (gate_out / (1.0 + jnp.exp(-gate_out)) * up_out).astype(BF16)
        for q in range(NY):
            pf[q, rows, :] = jnp.dot(
                hidden, down[:, 1024 * q : 1024 * q + 1024], preferred_element_type=F32
            ).astype(BF16)
        opposite = lax.rem(y + 2, NY)
        for g in members:
            for side, half, dy in ((0, first_half(g), 1), (1, second_half(g), 3)):
                one_copies[g, side] = remote(
                    pf.at[opposite, half], step1.at[half], one_s.at[g, side], one_r.at[g, side], along_y(dy)
                )

    def add_y(g):
        for side, half, dy in ((0, first_half(g), 1), (1, second_half(g), 3)):
            one_copies[g, side].wait_recv()
            to = lax.rem(y + dy, NY)
            pf[to, half, :] = (pf[to, half, :].astype(F32) + step1[half, :].astype(F32)).astype(BF16)
            rows = pl.ds(BASE[g], ROWS[g])
            two_copies[g, side] = remote(
                pf.at[to, rows], step2.at[side, rows], two_s.at[g, side], two_r.at[g, side], along_y(dy)
            )

    def give_back(g):
        two_copies[g, 0].wait_recv()
        two_copies[g, 1].wait_recv()
        parts = []
        for i in range(len(GROUPS[g])):
            rows = pl.ds(BASE[g] + 64 * i, 64)
            total = (
                pf[y, rows, :].astype(F32) + step2[0, rows, :].astype(F32) + step2[1, rows, :].astype(F32)
            ).astype(BF16)
            parts.append(
                jnp.concatenate([total[:, 128 * group : 128 * group + 128] for group in range(8)], axis=0)
            )
        stacked = jnp.concatenate(parts, axis=1) if len(parts) > 1 else parts[0]
        back_out[g][...] = jnp.dot(perm_back[...], stacked, preferred_element_type=F32).astype(BF16)
        for j in range(NEAR - 1, 0, -1):
            remote(
                back_out[g].at[pl.ds(16 * j, 16)], back_in[g].at[pl.ds(16 * j, 16)],
                back_s.at[g], back_r.at[g], behind(j),
            )
        back_in[g][0:16, :] = back_out[g][0:16, :]

    own = []

    def combine(g):
        wait_all(back_in[g], back_r.at[g])
        for i, k in enumerate(GROUPS[g]):
            part = jnp.dot(weighted[k], back_in[g][:, 128 * i : 128 * i + 128], preferred_element_type=F32)
            if k == 0:
                own.append(part)
            else:
                part_out[k] = part.astype(BF16)
                part_copies[k] = remote(
                    part_out.at[k], part_in.at[k], part_s.at[k], part_r.at[k], along_z(NZ - 4 * k)
                )

    stages = {
        "a": select_and_send, "p": permutations, "b": send_y, "c": forward_y, "w": weights,
        "h": send_far, "d": expert, "e": add_y, "f": give_back, "g": combine,
    }
    for stage, g in ORDER:
        stages[stage](g)

    result = own[0]
    for k in (1, 3, 2):
        part_copies[k].wait_recv()
        result += part_in[k].astype(F32)
    for group in range(8):
        out_ref[:, 128 * group : 128 * group + 128] = result[16 * group : 16 * group + 16, :].astype(BF16)

    for g in range(len(GROUPS)):
        wait_all(picked[g], near_s.at[g])
        wait_all(back_out[g], back_s.at[g])
        for i in range(4):
            y_copies[g, i].wait_send()
        for i in range(2):
            one_copies[g, i].wait_send()
            two_copies[g, i].wait_send()
    for k in range(1, 4):
        far_copies[k].wait_send()
        part_copies[k].wait_send()


def per_device(tokens, expert_ids, route_probs, gate_weight, up_weight, down_weight):
    vmem, dma = pltpu.VMEM, pltpu.SemaphoreType.DMA
    in_hbm = pl.BlockSpec(memory_space=pltpu.HBM)
    n = len(GROUPS)
    messages = [vmem((512, 128 * len(members)), BF16) for members in GROUPS]
    return pl.pallas_call(
        kernel,
        out_shape=jax.ShapeDtypeStruct((16, 1024), BF16),
        in_specs=[in_hbm] * 6,
        out_specs=pl.BlockSpec(memory_space=pltpu.VMEM),
        scratch_shapes=[
            vmem((16, 1024), BF16), vmem((8, 16), jnp.int32), vmem((8, 16), F32),
            vmem((192, 4096), BF16), vmem((192, 4096), BF16), vmem((192, 4096), BF16),
            vmem((4, 144, 128), BF16),
            vmem((512, 256), BF16), vmem((512, 512), BF16), vmem((512, 512), BF16),
            vmem((4, 128, 512), BF16),
            vmem((4, 256, 1024), BF16), vmem((4, 256, 1024), BF16),
            vmem((256, 1024), BF16), vmem((2, 256, 1024), BF16),
            vmem((4, 128, 128), BF16), vmem((4, 128, 128), BF16),
            dma((6,)), dma((4,)), dma((4,)), dma((n,)), dma((n,)),
            dma((n, 4)), dma((n, 4)), dma((n, 2)), dma((n, 2)), dma((n, 2)), dma((n, 2)),
            dma((n,)), dma((n,)), dma((4,)), dma((4,)),
        ] + messages * 4,
        compiler_params=pltpu.CompilerParams(
            collective_id=0, has_side_effects=True, vmem_limit_bytes=60 * 1024 * 1024
        ),
        cost_estimate=pl.CostEstimate(flops=1_300_000_000, bytes_accessed=5_000_000, transcendentals=50_000),
    )(tokens, expert_ids.T, route_probs.T, gate_weight, up_weight, down_weight)


def solution(mesh):
    placed = (
        P("expert", "hidden"),
        P("expert", None),
        P("expert", None),
        P("expert", "hidden", None),
        P("expert", "hidden", None),
        P("expert", "hidden", None),
    )
    return jax.shard_map(
        per_device, mesh=mesh, in_specs=placed, out_specs=P("expert", "hidden"), check_vma=False
    )
```

```python
import jax
import jax.numpy as jnp
from jax import lax
from jax.experimental import pallas as pl
from jax.experimental.pallas import tpu as pltpu
from jax.sharding import PartitionSpec as P

MESH = pl.DeviceIdType.MESH
BF16 = jnp.bfloat16
F32 = jnp.float32
NZ, NXC, NY = 16, 8, 4
NEAR = 32
GROUPS = ((0,), (1,), (3,), (2,))
BASE = (0, 64, 128, 192)
ROWS = (64, 64, 64, 64)
EXPERT = ((0,), (1,), (2,), (3,))
MIX = (2,)
ORDER = (
    ("h", 0), ("a", 0), ("p", 0), ("b", 0), ("i", 0), ("a", 1), ("a", 2), ("c", 0), ("b", 1), ("a", 3),
    ("b", 2), ("c", 1), ("w", 0), ("b", 3), ("c", 2), ("d", 1), ("c", 3), ("d", 2), ("f", 2), ("e", 1),
    ("d", 3), ("f", 1), ("d", 0), ("e", 3), ("g", 2), ("e", 0), ("g", 1), ("s", 2), ("f", 3), ("f", 0),
    ("g", 3), ("g", 0),
)


def kernel(tok_hbm, ids_hbm, prob_hbm, gate_hbm, up_hbm, down_hbm, out_ref, *scratch):
    (tok, ids_ref, prob_ref, gate, up, down, far, wanted, perm, perm_back, weighted, xf, pf, step1, step2,
     part_out, part_in, in_sem, far_s, far_r, near_s, near_r, y_s, y_r, one_s, one_r, two_s, two_r,
     back_s, back_r, part_s, part_r) = scratch[:32]
    n = len(GROUPS)
    picked, got, back_out, back_in = (scratch[32 + n * i : 32 + n * i + n] for i in range(4))
    all_out, all_in, all_s, all_r = scratch[32 + 4 * n :]

    e = lax.axis_index("expert")
    y = lax.axis_index("hidden")
    z, xc = lax.div(e, NXC), lax.rem(e, NXC)
    two = jnp.where(lax.rem(xc, 2) == 0, 2, NZ - 2)

    def along_y(dy):
        return (e, lax.rem(y + dy, NY))

    def along_z(dz):
        return (lax.rem(z + dz, NZ) * NXC + xc, y)

    z_bases = [lax.rem(z + dz, NZ) * NXC for dz in (0, 1, NZ - 1, two)]
    z_behind = lax.rem(z + NZ - two, NZ) * NXC
    xcs = [lax.rem(xc + d, NXC) for d in range(NXC)]

    def ahead(j):
        return (z_bases[j // 8] + xcs[j % 8], y)

    def behind(j):
        base = (z_bases[0], z_bases[2], z_bases[1], z_bases[3] if j % 2 else z_behind)[j // 8]
        return (base + xcs[-j % 8], y)

    barrier = pltpu.get_barrier_semaphore()
    partners = [along_z(4), along_z(12)]
    partners += [ahead(j) for j in range(NEAR - 1, 0, -1)]
    partners += [(z_behind + xcs[d], y) for d in range(0, NXC, 2)]
    partners += [along_y(k) for k in range(1, NY)]
    inputs = [
        pltpu.make_async_copy(src, dst, in_sem.at[i])
        for i, (src, dst) in enumerate((
            (tok_hbm, tok), (ids_hbm, ids_ref), (prob_hbm, prob_ref),
            (gate_hbm.at[0], gate), (up_hbm.at[0], up), (down_hbm.at[0], down),
        ))
    ]
    for i in range(3):
        inputs[i].start()
    for partner in partners:
        pl.semaphore_signal(barrier, inc=1, device_id=partner, device_id_type=MESH)

    def remote(src, dst, send, recv, device):
        copy = pltpu.make_async_remote_copy(
            src_ref=src, dst_ref=dst, send_sem=send, recv_sem=recv,
            device_id=device, device_id_type=MESH,
        )
        copy.start()
        return copy

    def iota(shape, axis):
        return lax.broadcasted_iota(jnp.int32, shape, axis)

    nt = (((1,), (1,)), ((), ()))

    for i in range(3):
        inputs[i].wait()
    for group in range(8):
        far[0, 16 * group : 16 * group + 16, :] = tok[:, 128 * group : 128 * group + 128]
    probs = prob_ref[...]
    share = probs / jnp.sum(probs, axis=0, keepdims=True)
    lists = jnp.concatenate([ids_ref[...].astype(F32), share, jnp.zeros((112, 16), F32)], axis=0).astype(BF16)
    same = (iota((16, 16), 0) == iota((16, 16), 1)).astype(F32).astype(BF16)
    far[0, 128:144, :] = lax.dot_general(same, lists, nt, preferred_element_type=F32).astype(BF16)

    row, col = iota((512, 256), 0), iota((512, 256), 1)
    hop = row >> 7
    dz = jnp.where(hop == 0, 0, jnp.where(hop == 1, 1, jnp.where(hop == 2, NZ - 1, two)))
    target = ((z + dz) & 15) * NXC + ((xc + (row >> 4)) & 7) + ((row & 1) << 7)
    wanted[...] = (target == col).astype(F32).astype(BF16)
    same_group = ((iota((512, 128), 0) & 15) >> 1) == (iota((512, 128), 1) >> 4)

    lane = iota((16, 128), 1).astype(F32)
    below = (iota((16, 16), 0) > iota((16, 16), 1)).astype(F32).astype(BF16)

    def turns(k, weigh):
        lists = far[k, 128:144, :].astype(F32)
        named, value = jnp.zeros((16, 128), F32), jnp.zeros((16, 128), F32)
        for q in range(8):
            hit = lists[:, q : q + 1] == lane
            named = jnp.where(hit, 1.0, named)
            if weigh:
                value = jnp.where(hit, lists[:, 8 + q : 9 + q], value)
        rank = jnp.dot(below, named.astype(BF16), preferred_element_type=F32)
        what = value if weigh else named
        return jnp.concatenate([jnp.where(rank == 0.0, what, 0.0), jnp.where(rank == 1.0, what, 0.0)], axis=1)

    def spread(block):
        return jnp.concatenate([block] * 8, axis=0).astype(BF16)

    def select(k, out):
        chosen = lax.dot_general(wanted[...], spread(turns(k, False)), nt, preferred_element_type=F32)
        chosen = jnp.where(same_group, chosen, 0.0).astype(BF16)
        out[...] = jnp.dot(chosen, far[k, 0:128, :], preferred_element_type=F32).astype(BF16)

    select(0, picked[0])
    pl.semaphore_wait(barrier, len(partners))

    far_copies = {}

    def send_far(_):
        for k in (1, 3):
            far_copies[k] = remote(far.at[0], far.at[k], far_s.at[k], far_r.at[k], along_z(4 * k))

    def forward_far(_):
        for k, rows, i in ((1, pl.ds(0, 80), 0), (3, pl.ds(80, 64), 2)):
            far_copies[k].wait_recv()
            far_copies[i] = remote(far.at[k, rows], far.at[2, rows], far_s.at[i], far_r.at[i], along_z(4 * k))

    for i in range(3, 6):
        inputs[i].start()

    def select_and_send(g):
        for i, k in enumerate(GROUPS[g]):
            if k == 2:
                far_copies[0].wait_recv()
                far_copies[2].wait_recv()
            if k:
                select(k, picked[g].at[:, pl.ds(128 * i, 128)])
        for j in range(NEAR - 1, 0, -1):
            remote(
                picked[g].at[pl.ds(16 * j, 16)], got[g].at[pl.ds(16 * j, 16)],
                near_s.at[g], near_r.at[g], ahead(j),
            )
        got[g][0:16, :] = picked[g][0:16, :]

    def permutations(_):
        a, b = iota((512, 512), 0), iota((512, 512), 1)
        perm[...] = (b == (((a & 63) >> 1) << 4) + ((a >> 6) << 1) + (a & 1)).astype(F32).astype(BF16)
        perm_back[...] = (a == (((b & 63) >> 1) << 4) + ((b >> 6) << 1) + (b & 1)).astype(F32).astype(BF16)

    def weights(_):
        for i in range(3, 6):
            inputs[i].wait()
        same = (iota((128, 512), 0) >> 4) == ((iota((128, 512), 1) & 15) >> 1)
        for k in range(4):
            full = lax.dot_general(spread(turns(k, True)), wanted[...], nt, preferred_element_type=F32)
            weighted[k] = jnp.where(same, full, 0.0).astype(BF16)

    def wait_all(ref, sem):
        rest = ref.at[pl.ds(16, 496)]
        pltpu.make_async_copy(rest, rest, sem).wait()

    y_copies, one_copies, two_copies, part_copies = {}, {}, {}, {}

    def send_y(g):
        wait_all(got[g], near_r.at[g])
        rows = jnp.dot(perm[...], got[g][...], preferred_element_type=F32).astype(BF16)
        for i in range(len(GROUPS[g])):
            first = BASE[g] + 64 * i
            for group in range(8):
                xf[y, first : first + 64, 128 * group : 128 * group + 128] = rows[
                    64 * group : 64 * group + 64, 128 * i : 128 * i + 128
                ]
        for i, half, dy in ((0, first_half(g), 1), (1, second_half(g), 3), (4, second_half(g), 1), (5, first_half(g), 3)):
            block = xf.at[y, half]
            y_copies[g, i] = remote(block, block, y_s.at[g, i], y_r.at[g, i], along_y(dy))

    def first_half(g):
        return pl.ds(BASE[g], ROWS[g] // 2)

    def second_half(g):
        return pl.ds(BASE[g] + ROWS[g] // 2, ROWS[g] // 2)

    def forward_y(g):
        y_copies[g, 0].wait_recv()
        block = xf.at[lax.rem(y + 3, NY), first_half(g)]
        y_copies[g, 2] = remote(block, block, y_s.at[g, 2], y_r.at[g, 2], along_y(1))
        y_copies[g, 1].wait_recv()
        block = xf.at[lax.rem(y + 1, NY), second_half(g)]
        y_copies[g, 3] = remote(block, block, y_s.at[g, 3], y_r.at[g, 3], along_y(3))

    def expert(which):
        members = EXPERT[which]
        for g in members:
            for i in range(2, 6):
                y_copies[g, i].wait_recv()
        count = sum(ROWS[g] for g in members)
        rows = pl.ds(BASE[members[0]], count)
        gate_out, up_out = jnp.zeros((count, 192), F32), jnp.zeros((count, 192), F32)
        for q in range(NY):
            x = xf[q, rows, :]
            gate_out += lax.dot_general(x, gate[:, 1024 * q : 1024 * q + 1024], nt, preferred_element_type=F32)
            up_out += lax.dot_general(x, up[:, 1024 * q : 1024 * q + 1024], nt, preferred_element_type=F32)
        hidden = (gate_out / (1.0 + jnp.exp(-gate_out)) * up_out).astype(BF16)
        for q in range(NY):
            pf[q, rows, :] = jnp.dot(
                hidden, down[:, 1024 * q : 1024 * q + 1024], preferred_element_type=F32
            ).astype(BF16)
        opposite = lax.rem(y + 2, NY)
        members = [g for g in members if g not in MIX]
        for g in members:
            for side, half, dy in ((0, first_half(g), 1), (1, second_half(g), 3)):
                one_copies[g, side] = remote(
                    pf.at[opposite, half], step1.at[half], one_s.at[g, side], one_r.at[g, side], along_y(dy)
                )
        for g in members:
            for side, half, dy in ((0, second_half(g), 1), (1, first_half(g), 3)):
                two_copies[g, 2 + side] = remote(
                    pf.at[lax.rem(y + dy, NY), half], step2.at[side, half],
                    two_s.at[g, 2 + side], two_r.at[g, 2 + side], along_y(dy),
                )

    def add_y(g):
        for side, half, dy in ((0, first_half(g), 1), (1, second_half(g), 3)):
            one_copies[g, side].wait_recv()
            to = lax.rem(y + dy, NY)
            pf[to, half, :] = (pf[to, half, :].astype(F32) + step1[half, :].astype(F32)).astype(BF16)
            two_copies[g, side] = remote(
                pf.at[to, half], step2.at[side, half], two_s.at[g, side], two_r.at[g, side], along_y(dy)
            )

    def stack(total):
        return jnp.concatenate([total[:, 128 * group : 128 * group + 128] for group in range(8)], axis=0)

    def give_back(g):
        rows = pl.ds(BASE[g], 64)
        if g in MIX:
            stacked = jnp.concatenate([stack(pf[q, rows, :]) for q in range(NY)], axis=1)
        else:
            for i in range(4):
                two_copies[g, i].wait_recv()
            total = pf[y, rows, :].astype(F32) + step2[0, rows, :].astype(F32) + step2[1, rows, :].astype(F32)
            stacked = stack(total.astype(BF16))
        back_out[g][...] = jnp.dot(perm_back[...], stacked, preferred_element_type=F32).astype(BF16)
        for j in range(NEAR - 1, 0, -1):
            remote(
                back_out[g].at[pl.ds(16 * j, 16)], back_in[g].at[pl.ds(16 * j, 16)],
                back_s.at[g], back_r.at[g], behind(j),
            )
        back_in[g][0:16, :] = back_out[g][0:16, :]

    own = []

    def send_part(k, part):
        part_out[k] = part.astype(BF16)
        part_copies[k] = remote(
            part_out.at[k], part_in.at[k], part_s.at[k], part_r.at[k], along_z(NZ - 4 * k)
        )

    def combine(g):
        wait_all(back_in[g], back_r.at[g])
        [k] = GROUPS[g]
        part = jnp.dot(weighted[k], back_in[g][...], preferred_element_type=F32)
        if g in MIX:
            for q in range(NY):
                all_out[g, q] = part[:, 128 * q : 128 * q + 128].astype(BF16)
            for dy in (2, 1, 3):
                all_copies[g, dy] = remote(
                    all_out.at[g, lax.rem(y + dy, NY)], all_in.at[g, dy], all_s.at[g, dy], all_r.at[g, dy],
                    along_y(dy),
                )
        elif k == 0:
            own.append(part)
        else:
            send_part(k, part)

    all_copies = {}

    def sum_y(g):
        part = all_out[g, y].astype(F32)
        for dy in (1, 3, 2):
            all_copies[g, dy].wait_recv()
            part += all_in[g, dy].astype(F32)
        send_part(GROUPS[g][0], part)

    stages = {
        "a": select_and_send, "p": permutations, "b": send_y, "c": forward_y, "w": weights,
        "s": sum_y, "h": send_far, "i": forward_far, "d": expert, "e": add_y, "f": give_back, "g": combine,
    }
    for stage, g in ORDER:
        stages[stage](g)

    result = own[0]
    for k in (1, 3, 2):
        part_copies[k].wait_recv()
        result += part_in[k].astype(F32)
    for group in range(8):
        out_ref[:, 128 * group : 128 * group + 128] = result[16 * group : 16 * group + 16, :].astype(BF16)

    for g in range(len(GROUPS)):
        wait_all(picked[g], near_s.at[g])
        wait_all(back_out[g], back_s.at[g])
        for i in range(6):
            y_copies[g, i].wait_send()
        if g in MIX:
            for dy in (1, 2, 3):
                all_copies[g, dy].wait_send()
        else:
            for i in range(2):
                one_copies[g, i].wait_send()
            for i in range(4):
                two_copies[g, i].wait_send()
    for k in range(4):
        far_copies[k].wait_send()
        if k:
            part_copies[k].wait_send()


def per_device(tokens, expert_ids, route_probs, gate_weight, up_weight, down_weight):
    vmem, dma = pltpu.VMEM, pltpu.SemaphoreType.DMA
    in_hbm = pl.BlockSpec(memory_space=pltpu.HBM)
    n = len(GROUPS)
    ahead = [vmem((512, 128), BF16)] * n
    back = [vmem((512, 512 if g in MIX else 128), BF16) for g in range(n)]
    return pl.pallas_call(
        kernel,
        out_shape=jax.ShapeDtypeStruct((16, 1024), BF16),
        in_specs=[in_hbm] * 6,
        out_specs=pl.BlockSpec(memory_space=pltpu.VMEM),
        scratch_shapes=[
            vmem((16, 1024), BF16), vmem((8, 16), jnp.int32), vmem((8, 16), F32),
            vmem((192, 4096), BF16), vmem((192, 4096), BF16), vmem((192, 4096), BF16),
            vmem((4, 144, 128), BF16),
            vmem((512, 256), BF16), vmem((512, 512), BF16), vmem((512, 512), BF16),
            vmem((4, 128, 512), BF16),
            vmem((4, 256, 1024), BF16), vmem((4, 256, 1024), BF16),
            vmem((256, 1024), BF16), vmem((2, 256, 1024), BF16),
            vmem((4, 128, 128), BF16), vmem((4, 128, 128), BF16),
            dma((6,)), dma((4,)), dma((4,)), dma((n,)), dma((n,)),
            dma((n, 6)), dma((n, 6)), dma((n, 2)), dma((n, 2)), dma((n, 4)), dma((n, 4)),
            dma((n,)), dma((n,)), dma((4,)), dma((4,)),
        ] + ahead * 2 + back * 2 + [vmem((n, 4, 128, 128), BF16)] * 2 + [dma((n, 4))] * 2,
        compiler_params=pltpu.CompilerParams(
            collective_id=0, has_side_effects=True, vmem_limit_bytes=60 * 1024 * 1024
        ),
        cost_estimate=pl.CostEstimate(flops=1_300_000_000, bytes_accessed=5_000_000, transcendentals=50_000),
    )(tokens, expert_ids.T, route_probs.T, gate_weight, up_weight, down_weight)


def solution(mesh):
    placed = (
        P("expert", "hidden"),
        P("expert", None),
        P("expert", None),
        P("expert", "hidden", None),
        P("expert", "hidden", None),
        P("expert", "hidden", None),
    )
    return jax.shard_map(
        per_device, mesh=mesh, in_specs=placed, out_specs=P("expert", "hidden"), check_vma=False
    )
```

```python
import jax
import jax.numpy as jnp
from jax import lax
from jax.experimental import pallas as pl
from jax.experimental.pallas import tpu as pltpu
from jax.sharding import PartitionSpec as P

MESH = pl.DeviceIdType.MESH
BF16 = jnp.bfloat16
F32 = jnp.float32
NZ, NXC, NY = 16, 8, 4
NEAR = 32
GROUPS = ((0,), (1,), (3,), (2,))
BASE = (0, 64, 128, 192)
ROWS = (64, 64, 64, 64)
EXPERT = ((0,), (1,), (2,), (3,))
MIX = (2,)
ORDER = (
    ("h", 0), ("a", 0), ("p", 0), ("i", 0), ("a", 1), ("b", 0), ("a", 2), ("c", 0), ("b", 1), ("a", 3),
    ("b", 2), ("c", 1), ("w", 0), ("b", 3), ("c", 2), ("d", 1), ("c", 3), ("d", 2), ("f", 2), ("e", 1),
    ("d", 3), ("d", 0), ("e", 3), ("f", 1), ("e", 0), ("g", 2), ("g", 1), ("s", 2), ("f", 3), ("f", 0),
    ("g", 3), ("g", 0),
)


def kernel(tok_hbm, ids_hbm, prob_hbm, gate_hbm, up_hbm, down_hbm, out_ref, *scratch):
    (tok, ids_ref, prob_ref, gate, up, down, far, wanted, perm, perm_back, weighted, xf, pf, step1, step2,
     part_out, part_in, in_sem, far_s, far_r, near_s, near_r, y_s, y_r, one_s, one_r, two_s, two_r,
     back_s, back_r, part_s, part_r) = scratch[:32]
    n = len(GROUPS)
    picked, got, back_out, back_in = (scratch[32 + n * i : 32 + n * i + n] for i in range(4))
    all_out, all_in, all_s, all_r = scratch[32 + 4 * n :]

    e = lax.axis_index("expert")
    y = lax.axis_index("hidden")
    z, xc = lax.div(e, NXC), lax.rem(e, NXC)
    two = jnp.where(lax.rem(xc, 2) == 0, 2, NZ - 2)

    def along_y(dy):
        return (e, lax.rem(y + dy, NY))

    def along_z(dz):
        return (lax.rem(z + dz, NZ) * NXC + xc, y)

    z_bases = [lax.rem(z + dz, NZ) * NXC for dz in (0, 1, NZ - 1, two)]
    z_behind = lax.rem(z + NZ - two, NZ) * NXC
    xcs = [lax.rem(xc + d, NXC) for d in range(NXC)]

    def ahead(j):
        return (z_bases[j // 8] + xcs[j % 8], y)

    def behind(j):
        base = (z_bases[0], z_bases[2], z_bases[1], z_bases[3] if j % 2 else z_behind)[j // 8]
        return (base + xcs[-j % 8], y)

    barrier = pltpu.get_barrier_semaphore()
    partners = [along_z(4), along_z(12)]
    partners += [ahead(j) for j in range(NEAR - 1, 0, -1)]
    partners += [(z_behind + xcs[d], y) for d in range(0, NXC, 2)]
    partners += [along_y(k) for k in range(1, NY)]
    inputs = [
        pltpu.make_async_copy(src, dst, in_sem.at[i])
        for i, (src, dst) in enumerate((
            (tok_hbm, tok), (ids_hbm, ids_ref), (prob_hbm, prob_ref),
            (gate_hbm.at[0], gate), (up_hbm.at[0], up), (down_hbm.at[0], down),
        ))
    ]
    for i in range(3):
        inputs[i].start()
    for partner in partners:
        pl.semaphore_signal(barrier, inc=1, device_id=partner, device_id_type=MESH)

    def remote(src, dst, send, recv, device):
        copy = pltpu.make_async_remote_copy(
            src_ref=src, dst_ref=dst, send_sem=send, recv_sem=recv,
            device_id=device, device_id_type=MESH,
        )
        copy.start()
        return copy

    def iota(shape, axis):
        return lax.broadcasted_iota(jnp.int32, shape, axis)

    nt = (((1,), (1,)), ((), ()))

    for i in range(3):
        inputs[i].wait()
    for group in range(8):
        far[0, 16 * group : 16 * group + 16, :] = tok[:, 128 * group : 128 * group + 128]
    probs = prob_ref[...]
    share = probs / jnp.sum(probs, axis=0, keepdims=True)
    lists = jnp.concatenate([ids_ref[...].astype(F32), share, jnp.zeros((112, 16), F32)], axis=0).astype(BF16)
    same = (iota((16, 16), 0) == iota((16, 16), 1)).astype(F32).astype(BF16)
    far[0, 128:144, :] = lax.dot_general(same, lists, nt, preferred_element_type=F32).astype(BF16)

    row, col = iota((512, 256), 0), iota((512, 256), 1)
    hop = row >> 7
    dz = jnp.where(hop == 0, 0, jnp.where(hop == 1, 1, jnp.where(hop == 2, NZ - 1, two)))
    target = ((z + dz) & 15) * NXC + ((xc + (row >> 4)) & 7) + ((row & 1) << 7)
    wanted[...] = (target == col).astype(F32).astype(BF16)
    same_group = ((iota((512, 128), 0) & 15) >> 1) == (iota((512, 128), 1) >> 4)

    lane = iota((16, 128), 1).astype(F32)
    below = (iota((16, 16), 0) > iota((16, 16), 1)).astype(F32).astype(BF16)

    def turns(k, weigh):
        lists = far[k, 128:144, :].astype(F32)
        named, value = jnp.zeros((16, 128), F32), jnp.zeros((16, 128), F32)
        for q in range(8):
            hit = lists[:, q : q + 1] == lane
            named = jnp.where(hit, 1.0, named)
            if weigh:
                value = jnp.where(hit, lists[:, 8 + q : 9 + q], value)
        rank = jnp.dot(below, named.astype(BF16), preferred_element_type=F32)
        what = value if weigh else named
        return jnp.concatenate([jnp.where(rank == 0.0, what, 0.0), jnp.where(rank == 1.0, what, 0.0)], axis=1)

    def spread(block):
        return jnp.concatenate([block] * 8, axis=0).astype(BF16)

    def select(k, out):
        chosen = lax.dot_general(wanted[...], spread(turns(k, False)), nt, preferred_element_type=F32)
        chosen = jnp.where(same_group, chosen, 0.0).astype(BF16)
        out[...] = jnp.dot(chosen, far[k, 0:128, :], preferred_element_type=F32).astype(BF16)

    select(0, picked[0])
    pl.semaphore_wait(barrier, len(partners))

    far_copies = {}

    def send_far(_):
        for k in (1, 3):
            far_copies[k] = remote(far.at[0], far.at[k], far_s.at[k], far_r.at[k], along_z(4 * k))

    def forward_far(_):
        for k, rows, i in ((1, pl.ds(0, 80), 0), (3, pl.ds(80, 64), 2)):
            far_copies[k].wait_recv()
            far_copies[i] = remote(far.at[k, rows], far.at[2, rows], far_s.at[i], far_r.at[i], along_z(4 * k))

    for i in range(3, 6):
        inputs[i].start()

    def select_and_send(g):
        for i, k in enumerate(GROUPS[g]):
            if k == 2:
                far_copies[0].wait_recv()
                far_copies[2].wait_recv()
            if k:
                select(k, picked[g].at[:, pl.ds(128 * i, 128)])
        for j in range(NEAR - 1, 0, -1):
            remote(
                picked[g].at[pl.ds(16 * j, 16)], got[g].at[pl.ds(16 * j, 16)],
                near_s.at[g], near_r.at[g], ahead(j),
            )
        got[g][0:16, :] = picked[g][0:16, :]

    def permutations(_):
        a, b = iota((512, 512), 0), iota((512, 512), 1)
        perm[...] = (b == (((a & 63) >> 1) << 4) + ((a >> 6) << 1) + (a & 1)).astype(F32).astype(BF16)
        perm_back[...] = (a == (((b & 63) >> 1) << 4) + ((b >> 6) << 1) + (b & 1)).astype(F32).astype(BF16)

    def weights(_):
        for i in range(3, 6):
            inputs[i].wait()
        same = (iota((128, 512), 0) >> 4) == ((iota((128, 512), 1) & 15) >> 1)
        for k in range(4):
            full = lax.dot_general(spread(turns(k, True)), wanted[...], nt, preferred_element_type=F32)
            weighted[k] = jnp.where(same, full, 0.0).astype(BF16)

    def wait_all(ref, sem):
        rest = ref.at[pl.ds(16, 496)]
        pltpu.make_async_copy(rest, rest, sem).wait()

    y_copies, one_copies, two_copies, part_copies = {}, {}, {}, {}

    def send_y(g):
        wait_all(got[g], near_r.at[g])
        rows = jnp.dot(perm[...], got[g][...], preferred_element_type=F32).astype(BF16)
        for i in range(len(GROUPS[g])):
            first = BASE[g] + 64 * i
            for group in range(8):
                xf[y, first : first + 64, 128 * group : 128 * group + 128] = rows[
                    64 * group : 64 * group + 64, 128 * i : 128 * i + 128
                ]
        for i, half, dy in ((0, first_half(g), 1), (1, second_half(g), 3), (4, second_half(g), 1), (5, first_half(g), 3)):
            block = xf.at[y, half]
            y_copies[g, i] = remote(block, block, y_s.at[g, i], y_r.at[g, i], along_y(dy))

    def first_half(g):
        return pl.ds(BASE[g], ROWS[g] // 2)

    def second_half(g):
        return pl.ds(BASE[g] + ROWS[g] // 2, ROWS[g] // 2)

    def forward_y(g):
        y_copies[g, 0].wait_recv()
        block = xf.at[lax.rem(y + 3, NY), first_half(g)]
        y_copies[g, 2] = remote(block, block, y_s.at[g, 2], y_r.at[g, 2], along_y(1))
        y_copies[g, 1].wait_recv()
        block = xf.at[lax.rem(y + 1, NY), second_half(g)]
        y_copies[g, 3] = remote(block, block, y_s.at[g, 3], y_r.at[g, 3], along_y(3))

    def expert(which):
        members = EXPERT[which]
        for g in members:
            for i in range(2, 6):
                y_copies[g, i].wait_recv()
        count = sum(ROWS[g] for g in members)
        rows = pl.ds(BASE[members[0]], count)
        gate_out, up_out = jnp.zeros((count, 192), F32), jnp.zeros((count, 192), F32)
        for q in range(NY):
            x = xf[q, rows, :]
            gate_out += lax.dot_general(x, gate[:, 1024 * q : 1024 * q + 1024], nt, preferred_element_type=F32)
            up_out += lax.dot_general(x, up[:, 1024 * q : 1024 * q + 1024], nt, preferred_element_type=F32)
        hidden = (gate_out / (1.0 + jnp.exp(-gate_out)) * up_out).astype(BF16)
        for q in range(NY):
            pf[q, rows, :] = jnp.dot(
                hidden, down[:, 1024 * q : 1024 * q + 1024], preferred_element_type=F32
            ).astype(BF16)
        opposite = lax.rem(y + 2, NY)
        members = [g for g in members if g not in MIX]
        for g in members:
            for side, half, dy in ((0, first_half(g), 1), (1, second_half(g), 3)):
                one_copies[g, side] = remote(
                    pf.at[opposite, half], step1.at[half], one_s.at[g, side], one_r.at[g, side], along_y(dy)
                )
        for g in members:
            for side, half, dy in ((0, second_half(g), 1), (1, first_half(g), 3)):
                two_copies[g, 2 + side] = remote(
                    pf.at[lax.rem(y + dy, NY), half], step2.at[side, half],
                    two_s.at[g, 2 + side], two_r.at[g, 2 + side], along_y(dy),
                )

    def add_y(g):
        for side, half, dy in ((0, first_half(g), 1), (1, second_half(g), 3)):
            one_copies[g, side].wait_recv()
            to = lax.rem(y + dy, NY)
            pf[to, half, :] = (pf[to, half, :].astype(F32) + step1[half, :].astype(F32)).astype(BF16)
            two_copies[g, side] = remote(
                pf.at[to, half], step2.at[side, half], two_s.at[g, side], two_r.at[g, side], along_y(dy)
            )

    def stack(total):
        return jnp.concatenate([total[:, 128 * group : 128 * group + 128] for group in range(8)], axis=0)

    def give_back(g):
        rows = pl.ds(BASE[g], 64)
        if g in MIX:
            stacked = jnp.concatenate([stack(pf[q, rows, :]) for q in range(NY)], axis=1)
        else:
            for i in range(4):
                two_copies[g, i].wait_recv()
            total = pf[y, rows, :].astype(F32) + step2[0, rows, :].astype(F32) + step2[1, rows, :].astype(F32)
            stacked = stack(total.astype(BF16))
        back_out[g][...] = jnp.dot(perm_back[...], stacked, preferred_element_type=F32).astype(BF16)
        for j in range(NEAR - 1, 0, -1):
            remote(
                back_out[g].at[pl.ds(16 * j, 16)], back_in[g].at[pl.ds(16 * j, 16)],
                back_s.at[g], back_r.at[g], behind(j),
            )
        back_in[g][0:16, :] = back_out[g][0:16, :]

    own = []

    def send_part(k, part):
        part_out[k] = part.astype(BF16)
        part_copies[k] = remote(
            part_out.at[k], part_in.at[k], part_s.at[k], part_r.at[k], along_z(NZ - 4 * k)
        )

    def combine(g):
        wait_all(back_in[g], back_r.at[g])
        [k] = GROUPS[g]
        part = jnp.dot(weighted[k], back_in[g][...], preferred_element_type=F32)
        if g in MIX:
            for q in range(NY):
                all_out[g, q] = part[:, 128 * q : 128 * q + 128].astype(BF16)
            for dy in (2, 1, 3):
                all_copies[g, dy] = remote(
                    all_out.at[g, lax.rem(y + dy, NY)], all_in.at[g, dy], all_s.at[g, dy], all_r.at[g, dy],
                    along_y(dy),
                )
        elif k == 0:
            own.append(part)
        else:
            send_part(k, part)

    all_copies = {}

    def sum_y(g):
        part = all_out[g, y].astype(F32)
        for dy in (1, 3, 2):
            all_copies[g, dy].wait_recv()
            part += all_in[g, dy].astype(F32)
        send_part(GROUPS[g][0], part)

    stages = {
        "a": select_and_send, "p": permutations, "b": send_y, "c": forward_y, "w": weights,
        "s": sum_y, "h": send_far, "i": forward_far, "d": expert, "e": add_y, "f": give_back, "g": combine,
    }
    for stage, g in ORDER:
        stages[stage](g)

    result = own[0]
    for k in (1, 3, 2):
        part_copies[k].wait_recv()
        result += part_in[k].astype(F32)
    for group in range(8):
        out_ref[:, 128 * group : 128 * group + 128] = result[16 * group : 16 * group + 16, :].astype(BF16)

    for g in range(len(GROUPS)):
        wait_all(picked[g], near_s.at[g])
        wait_all(back_out[g], back_s.at[g])
        for i in range(6):
            y_copies[g, i].wait_send()
        if g in MIX:
            for dy in (1, 2, 3):
                all_copies[g, dy].wait_send()
        else:
            for i in range(2):
                one_copies[g, i].wait_send()
            for i in range(4):
                two_copies[g, i].wait_send()
    for k in range(4):
        far_copies[k].wait_send()
        if k:
            part_copies[k].wait_send()


def per_device(tokens, expert_ids, route_probs, gate_weight, up_weight, down_weight):
    vmem, dma = pltpu.VMEM, pltpu.SemaphoreType.DMA
    in_hbm = pl.BlockSpec(memory_space=pltpu.HBM)
    n = len(GROUPS)
    ahead = [vmem((512, 128), BF16)] * n
    back = [vmem((512, 512 if g in MIX else 128), BF16) for g in range(n)]
    return pl.pallas_call(
        kernel,
        out_shape=jax.ShapeDtypeStruct((16, 1024), BF16),
        in_specs=[in_hbm] * 6,
        out_specs=pl.BlockSpec(memory_space=pltpu.VMEM),
        scratch_shapes=[
            vmem((16, 1024), BF16), vmem((8, 16), jnp.int32), vmem((8, 16), F32),
            vmem((192, 4096), BF16), vmem((192, 4096), BF16), vmem((192, 4096), BF16),
            vmem((4, 144, 128), BF16),
            vmem((512, 256), BF16), vmem((512, 512), BF16), vmem((512, 512), BF16),
            vmem((4, 128, 512), BF16),
            vmem((4, 256, 1024), BF16), vmem((4, 256, 1024), BF16),
            vmem((256, 1024), BF16), vmem((2, 256, 1024), BF16),
            vmem((4, 128, 128), BF16), vmem((4, 128, 128), BF16),
            dma((6,)), dma((4,)), dma((4,)), dma((n,)), dma((n,)),
            dma((n, 6)), dma((n, 6)), dma((n, 2)), dma((n, 2)), dma((n, 4)), dma((n, 4)),
            dma((n,)), dma((n,)), dma((4,)), dma((4,)),
        ] + ahead * 2 + back * 2 + [vmem((n, 4, 128, 128), BF16)] * 2 + [dma((n, 4))] * 2,
        compiler_params=pltpu.CompilerParams(
            collective_id=0, has_side_effects=True, vmem_limit_bytes=60 * 1024 * 1024
        ),
        cost_estimate=pl.CostEstimate(flops=1_300_000_000, bytes_accessed=5_000_000, transcendentals=50_000),
    )(tokens, expert_ids.T, route_probs.T, gate_weight, up_weight, down_weight)


def solution(mesh):
    placed = (
        P("expert", "hidden"),
        P("expert", None),
        P("expert", None),
        P("expert", "hidden", None),
        P("expert", "hidden", None),
        P("expert", "hidden", None),
    )
    return jax.shard_map(
        per_device, mesh=mesh, in_specs=placed, out_specs=P("expert", "hidden"), check_vma=False
    )
```
